32 devices in a mesh: grp: 2 (over y), ex: 4 (over x, core), row: 4 (over z).
Axes of the slice: x: 2, y: 2, z: 4, core: 2. Of those that a mesh axis runs over, the one named last changes fastest.
Arguments:
- hidden: bfloat16 [16384, 28672], P(('grp', 'ex'), 'row'), parts along dimension 0, may hold values from -6 to 6
- out_grads: bfloat16 [16384, 8192], P(('grp', 'ex'), 'row'), parts along dimension 0, may hold values from -6 to 6
- proj_hidden: bfloat16 [28672, 512], P('row'), may hold values from -0.03125 to 0.03125
- proj_grads: bfloat16 [8192, 512], P('row'), may hold values from -0.0625 to 0.0625
- lengths: int32 [128], P('grp'), parts along dimension 0, may hold values from 1 to 512, 8192 in all
- owner_slots: int32 [128], P('grp'), parts along dimension 0, may hold values from 0 to 63, each once
Outputs:
- features: float32 [128, 512], P(('grp', 'ex')), parts along dimension 0
The draws below stay inside these ranges and needn't reach their ends.
There are 2 independent parts, one for each index of `grp`. The reference program is written for one: setup_inputs(seed, part) draws one part's arguments, and reference() takes and returns one part's arrays. A program takes and returns all parts, laid end to end along the dimension named above; an argument that names none is the same for every part. Nothing has to cross between parts.
Inputs may be any that keep to these rules, and one draw needn't show every extreme that they name: `lengths`: they sum to 8192; some example has exactly 512 tokens. `owner_slots`: each of the 64 rows is named once.
All inputs are finite; a program needn't handle non-finite values.
Results may differ from the reference program's by a relative error of at most 0.0029.
Values may be sent and summed in bfloat16 or wider, within the bound.
A program may use at most 128 MiB of HBM per device.

```python
import math
import jax
import jax.numpy as jnp
import numpy as np
from jax import lax

D = 8192
FF = 28672
K = 512
MOST = 512
TOKENS = 8192
EXAMPLES = 64


def with_spikes(array, rng, source, target, shards_of, factor):
    owner, partner = [(jnp.arange(array.shape[dim]) // (array.shape[dim] // shards_of)).reshape([-1 if axis == dim else 1 for axis in range(array.ndim)]) for dim in (source, target)]
    chosen = jax.random.permutation(rng, shards_of)[partner]
    strong = (owner == chosen) | (owner == (partner + shards_of // 2) % shards_of)
    return jnp.where(strong, factor * array, array)


def level_of(rng, shape, pieces, smallest, high):
    def one(axis_at, blocks):
        draws = jax.random.uniform(jax.random.fold_in(jax.random.fold_in(rng, 6), axis_at), (blocks,), jnp.float32, smallest / len(pieces), high / len(pieces))
        return jnp.repeat(jnp.exp(draws), shape[axis_at] // blocks).reshape((-1,) + (1,) * (len(shape) - axis_at - 1))

    factor_of = one(*pieces[0])
    for cut in pieces[1:]:
        factor_of = factor_of * one(*cut)
    return factor_of


def profile(count, total, limit, skew):
    loads = [(1 << 20) // math.isqrt(grade ** skew) + 1 for grade in range(2, count + 1)]
    spare, given = total - limit - (count - 1), [1] * (count - 1)
    while spare > 0:
        free = [i for i in range(count - 1) if given[i] < limit]
        mass, left = sum([loads[i] for i in free]), spare
        for i in free:
            addition = min(limit - given[i], max(1, left * loads[i] // mass), spare)
            given[i] = given[i] + addition
            spare = spare - addition
    return np.array([limit] + given)


def uneven_parts(rng, amount, total, limit, slope):
    if amount == 2:
        one = jax.random.randint(rng, (), max(1, total - limit), min(limit, total - 1) + 1)
        return jnp.stack([one, total - one])
    sizes = jnp.asarray(profile(amount, total, limit, slope), jnp.int32)
    pairs = (amount - 1) // 2
    giver, taker = sizes[1:1 + 2 * pairs:2], sizes[2:2 + 2 * pairs:2]
    slack = jnp.minimum(giver - 1, limit - taker)
    shifted = jax.random.randint(jax.random.fold_in(rng, 1), (pairs,), 0, 1 << 20) % (slack + 1)
    sizes = sizes.at[1:1 + 2 * pairs:2].set(giver - shifted).at[2:2 + 2 * pairs:2].set(taker + shifted)
    return sizes[jax.random.permutation(jax.random.fold_in(rng, 2), amount)]


def gaussian(stream_key, dims, scale, most, shards=(), kind=jnp.bfloat16):
    loudness = level_of(stream_key, dims, shards, -0.22, 0.18) if shards else 1.0
    entries = jax.random.normal(stream_key, dims, jnp.float32) * scale * loudness
    return jnp.minimum(jnp.maximum(entries, -most), most).astype(kind)


def noise_with(own_key, extent, scale, most, pieces, heavy, kind=jnp.bfloat16):
    values = scale * jax.random.normal(own_key, extent, jnp.float32)
    if pieces:
        values = values * level_of(own_key, extent, pieces, -0.22, 0.18)
    return jnp.clip(with_spikes(values, jax.random.fold_in(own_key, 3), *heavy), -most, most).astype(kind)


def setup_inputs(seed: int = 0, part: int = 0) -> dict:
    key_of = jax.random.split(jax.random.key(seed), 7)
    part_splits = jax.random.split(jax.random.fold_in(key_of[6], part), 7)
    return {
        "hidden": gaussian(part_splits[0], (TOKENS, FF), 1.0, 6.0, ((0, 4), (1, 4))),
        "out_grads": noise_with(part_splits[1], (TOKENS, D), 1.0, 6.0, ((0, 4), (1, 4)), (1, 0, 4, 2.0)),
        "proj_hidden": gaussian(key_of[2], (FF, K), FF ** -0.5, 0.03125, ((0, 4),)),
        "proj_grads": gaussian(key_of[3], (D, K), D ** -0.5, 0.0625, ((0, 4),)),
        "lengths": uneven_parts(part_splits[4], EXAMPLES, TOKENS, MOST, 2).astype(jnp.int32),
        "owner_slots": jax.random.permutation(part_splits[5], EXAMPLES).astype(jnp.int32),
    }


def reference(hidden, out_grads, proj_hidden, proj_grads, lengths, owner_slots):
    hid_proj = jnp.dot(hidden, proj_hidden, preferred_element_type=jnp.float32)
    grad_proj = jnp.dot(out_grads, proj_grads, preferred_element_type=jnp.float32).astype(jnp.bfloat16)
    doc_ends = jnp.cumsum(lengths).astype(jnp.int32)
    doc_starts = (doc_ends - lengths).astype(jnp.int32)
    position = jnp.arange(TOKENS, dtype=jnp.int32)
    member = ((position[:, None] >= doc_starts[None, :]) & (position[:, None] < doc_ends[None, :])).astype(jnp.float32)
    product = hid_proj * grad_proj.astype(jnp.float32)
    summed = jnp.dot(member.T, product, precision=lax.Precision.HIGHEST)
    phi = summed / jnp.sqrt(lengths.astype(jnp.float32))[:, None]
    return jnp.zeros((EXAMPLES, K), jnp.float32).at[owner_slots].set(phi)
```

```python
import functools

import jax
import jax.numpy as jnp
from jax import lax
from jax.experimental import pallas as pl
from jax.experimental.pallas import tpu as pltpu
from jax.sharding import PartitionSpec as P

MESH = pl.DeviceIdType.MESH
TILE = 256
CHUNK = 64
PER = TILE // CHUNK
RING = 8
LEAD = 4
PEER_LAG = 2
LAG = 4


def sums_kernel(
    ex_count, len_ref, own_ref, og_hbm, pg_hbm, hid_hbm, ph_hbm, out_ref,
    og, pg, ph, hid, grad, hidp, near_out, peer_out, near_in, peer_in,
    lo, hi, acc, block, got_ex, got_row,
    pg_sem, og_sem, ph_sem, hid_sem,
    near_send, near_recv, peer_send, peer_recv, ex_send, ex_recv, row_send, row_recv,
):
    ex = lax.axis_index("ex")
    row = lax.axis_index("row")
    tokens = og_hbm.shape[0]
    tiles = tokens // TILE
    chunks = tokens // CHUNK
    examples = len_ref.shape[1]
    per_owner = examples // ex_count
    depth = ph_hbm.shape[0] // PER
    near = row + 1 - 2 * (row % 2)
    peer = 3 - row
    is_mid = (row == 1) | (row == 2)
    is_end = (row == 0) | (row == 3)

    def load_og(i):
        return pltpu.make_async_copy(
            og_hbm.at[pl.ds(pl.multiple_of(i * TILE, TILE), TILE)], og.at[i], og_sem.at[i]
        )

    def load_ph(k):
        return pltpu.make_async_copy(
            ph_hbm.at[pl.ds(pl.multiple_of(k * depth, depth), depth)], ph.at[k], ph_sem.at[k]
        )

    def load_hid(s):
        i, k = s // PER, s % PER
        return pltpu.make_async_copy(
            hid_hbm.at[
                pl.ds(pl.multiple_of(i * TILE, TILE), TILE),
                pl.ds(pl.multiple_of(k * depth, 128), depth),
            ],
            hid.at[s % RING],
            hid_sem.at[s % RING],
        )

    def near_copy(c):
        return pltpu.make_async_remote_copy(
            src_ref=near_out.at[c], dst_ref=near_in.at[c],
            send_sem=near_send.at[c], recv_sem=near_recv.at[c],
            device_id={"row": near}, device_id_type=MESH,
        )

    def peer_copy(c):
        return pltpu.make_async_remote_copy(
            src_ref=peer_out.at[c], dst_ref=peer_in.at[c],
            send_sem=peer_send.at[c], recv_sem=peer_recv.at[c],
            device_id={"row": peer}, device_id_type=MESH,
        )

    pg_copy = pltpu.make_async_copy(pg_hbm, pg, pg_sem)
    pg_copy.start()
    load_og(0).start()
    load_og(1).start()
    barrier = pltpu.get_barrier_semaphore()
    for d in range(1, ex_count):
        pl.semaphore_signal(barrier, inc=1, device_id={"ex": (ex + d) % ex_count}, device_id_type=MESH)
    for d in range(1, 4):
        pl.semaphore_signal(barrier, inc=1, device_id={"row": (row + d) % 4}, device_id_type=MESH)
    for k in range(PER):
        load_ph(k).start()
        load_hid(k).start()
    for i in range(2, tiles):
        load_og(i).start()
    for s in range(PER, RING):
        load_hid(s).start()

    length = len_ref[...].astype(jnp.float32)
    r = lax.broadcasted_iota(jnp.int32, (examples, examples), 0)
    c = lax.broadcasted_iota(jnp.int32, (examples, examples), 1)
    ends = jnp.sum(jnp.where(c <= r, length, 0.0), axis=1, keepdims=True)
    ends = jnp.sum(jnp.where(r == c, ends, 0.0), axis=0, keepdims=True)
    starts = ends - length
    mine = own_ref[...] == r
    hi[...] = jnp.broadcast_to(
        jnp.sum(jnp.where(mine, ends, 0.0), axis=1, keepdims=True), hi.shape
    )
    lo[...] = jnp.broadcast_to(
        jnp.sum(jnp.where(mine, starts, 0.0), axis=1, keepdims=True), lo.shape
    )
    acc[...] = jnp.zeros_like(acc)

    def grad_tile(i):
        load_og(i).wait()
        g = jnp.dot(og[i], pg[...], preferred_element_type=jnp.float32)
        g = g.reshape(PER, CHUNK, g.shape[-1])
        at = pl.ds(pl.multiple_of(i * PER, PER), PER)
        grad[at] = g

        @pl.when(is_end)
        def _():
            near_out[at] = g.astype(jnp.bfloat16)

    pg_copy.wait()
    grad_tile(0)
    pl.semaphore_wait(barrier, ex_count - 1 + 3)

    @pl.when(is_end)
    def _():
        for m in range(LEAD):
            near_copy(m).start()

    grad_tile(1)

    def add_up(m, total):
        product = total * hidp[m]
        high = product.astype(jnp.bfloat16)
        low = (product - high.astype(jnp.float32)).astype(jnp.bfloat16)
        position = (
            ex * tokens + m * CHUNK + lax.broadcasted_iota(jnp.int32, (examples, CHUNK), 1)
        ).astype(jnp.float32)
        member = jnp.where(
            (position >= lo[:, :CHUNK]) & (position < hi[:, :CHUNK]), 1.0, 0.0
        ).astype(jnp.bfloat16)
        acc[...] += jnp.dot(member, high, preferred_element_type=jnp.float32) + jnp.dot(
            member, low, preferred_element_type=jnp.float32
        )

    def step(s, carry):
        i, k = s // PER, s % PER

        @pl.when(s < chunks)
        def _():
            load_hid(s).wait()

            @pl.when(i == 0)
            def _():
                load_ph(k).wait()

            h = jnp.dot(hid[s % RING], ph[k], preferred_element_type=jnp.float32)
            h = h.reshape(PER, CHUNK, h.shape[-1])
            at = pl.ds(pl.multiple_of(i * PER, PER), PER)

            @pl.when(k == 0)
            def _():
                hidp[at] = h

            @pl.when(k > 0)
            def _():
                hidp[at] += h

            @pl.when(s + RING < chunks)
            def _():
                load_hid(s + RING).start()

        @pl.when((k == 0) & (i + 2 < tiles))
        def _():
            grad_tile(i + 2)

        @pl.when(is_end & (s + LEAD < chunks))
        def _():
            near_copy(s + LEAD).start()

        @pl.when(is_mid & (s < chunks))
        def _():
            near_copy(s).wait_recv()
            peer_out[s] = (near_in[s].astype(jnp.float32) + grad[s]).astype(jnp.bfloat16)
            peer_copy(s).start()

        @pl.when(is_mid & (s >= PEER_LAG) & (s < chunks + PEER_LAG))
        def _():
            m = s - PEER_LAG
            peer_copy(m).wait_recv()
            near_out[m] = (peer_in[m].astype(jnp.float32) + grad[m]).astype(jnp.bfloat16)
            near_copy(m).start()

        @pl.when(is_end & (s >= LAG))
        def _():
            m = s - LAG
            near_copy(m).wait_recv()
            add_up(m, grad[m] + near_in[m].astype(jnp.float32))

        @pl.when(is_mid & (s >= LAG))
        def _():
            m = s - LAG
            add_up(
                m, grad[m] + near_in[m].astype(jnp.float32) + peer_in[m].astype(jnp.float32)
            )

        return carry

    lax.fori_loop(0, chunks + LAG, step, 0)

    acc[...] = acc[...] / jnp.sqrt(hi[:, :1] - lo[:, :1])

    def ex_copy(d):
        to = (ex + d) % ex_count
        return pltpu.make_async_remote_copy(
            src_ref=acc.at[pl.ds(pl.multiple_of(to * per_owner, per_owner), per_owner)],
            dst_ref=got_ex.at[d - 1],
            send_sem=ex_send.at[d - 1], recv_sem=ex_recv.at[d - 1],
            device_id={"ex": to}, device_id_type=MESH,
        )

    for d in range(1, ex_count):
        ex_copy(d).start()
    total = acc[pl.ds(pl.multiple_of(ex * per_owner, per_owner), per_owner)]
    for d in range(1, ex_count):
        ex_copy(d).wait_recv()
        total = total + got_ex[d - 1]
    block[...] = total

    def row_copy(d):
        return pltpu.make_async_remote_copy(
            src_ref=block, dst_ref=got_row.at[row],
            send_sem=row_send.at[d - 1], recv_sem=row_recv.at[row],
            device_id={"row": (row + d) % 4}, device_id_type=MESH,
        )

    for d in range(1, 4):
        row_copy(d).start()
    for d in range(1, 4):
        source = (row + d) % 4
        pltpu.make_async_remote_copy(
            src_ref=block, dst_ref=got_row.at[source],
            send_sem=row_send.at[d - 1], recv_sem=row_recv.at[source],
            device_id={"row": source}, device_id_type=MESH,
        ).wait_recv()
    got_row[row] = total
    out_ref[...] = (got_row[0] + got_row[1]) + (got_row[2] + got_row[3])

    for d in range(1, ex_count):
        ex_copy(d).wait_send()
    for d in range(1, 4):
        row_copy(d).wait_send()

    def drain(m, carry):
        near_copy(m).wait_send()

        @pl.when(is_mid)
        def _():
            peer_copy(m).wait_send()

        return carry

    lax.fori_loop(0, chunks, drain, 0)


def with_kernel(ex_count, hidden, out_grads, proj_hidden, proj_grads, lengths, owner_slots):
    tokens, units = hidden.shape
    features = out_grads.shape[1]
    k_dim = proj_hidden.shape[1]
    examples = lengths.shape[0]
    per_owner = examples // ex_count
    tiles, chunks = tokens // TILE, tokens // CHUNK
    bf16, f32 = jnp.bfloat16, jnp.float32
    dma = pltpu.SemaphoreType.DMA
    messages = pltpu.VMEM((chunks, CHUNK, k_dim), bf16)
    return pl.pallas_call(
        functools.partial(sums_kernel, ex_count),
        out_shape=jax.ShapeDtypeStruct((per_owner, k_dim), f32),
        in_specs=[pl.BlockSpec(memory_space=pltpu.VMEM)] * 2
        + [pl.BlockSpec(memory_space=pl.ANY)] * 4,
        out_specs=pl.BlockSpec(memory_space=pltpu.VMEM),
        scratch_shapes=[
            pltpu.VMEM((tiles, TILE, features), bf16),
            pltpu.VMEM((features, k_dim), bf16),
            pltpu.VMEM((PER, units // PER, k_dim), bf16),
            pltpu.VMEM((RING, TILE, units // PER), bf16),
            pltpu.VMEM((chunks, CHUNK, k_dim), f32),
            pltpu.VMEM((chunks, CHUNK, k_dim), f32),
            messages, messages, messages, messages,
            pltpu.VMEM((examples, 128), f32),
            pltpu.VMEM((examples, 128), f32),
            pltpu.VMEM((examples, k_dim), f32),
            pltpu.VMEM((per_owner, k_dim), f32),
            pltpu.VMEM((ex_count - 1, per_owner, k_dim), f32),
            pltpu.VMEM((4, per_owner, k_dim), f32),
            dma, dma((tiles,)), dma((PER,)), dma((RING,)),
            dma((chunks,)), dma((chunks,)), dma((chunks,)), dma((chunks,)),
            dma((ex_count - 1,)), dma((ex_count - 1,)), dma((3,)), dma((4,)),
        ],
        compiler_params=pltpu.CompilerParams(
            collective_id=0, has_side_effects=True, vmem_limit_bytes=56 * 2**20
        ),
    )(lengths[None, :], owner_slots[None, :], out_grads, proj_grads, hidden, proj_hidden)


def with_collectives(hidden, out_grads, proj_hidden, proj_grads, lengths, owner_slots):
    tok_count = hidden.shape[0]
    example_count = lengths.shape[0]
    shares = lax.psum_scatter(
        jnp.dot(out_grads, proj_grads, preferred_element_type=jnp.float32),
        "row",
        scatter_dimension=0,
        tiled=True,
    )
    shares_low = shares.astype(jnp.bfloat16)
    hid_part = jnp.dot(hidden, proj_hidden, preferred_element_type=jnp.float32)
    doc_ends = jnp.cumsum(lengths)
    doc_starts = doc_ends - lengths
    grad_proj = lax.all_gather(shares_low, "row", axis=0, tiled=True)
    product = hid_part * grad_proj.astype(jnp.float32)
    position = lax.axis_index("ex") * tok_count + jnp.arange(tok_count, dtype=jnp.int32)
    slot_ids = jnp.arange(example_count, dtype=jnp.int32)
    placing = slot_ids[:, None] == owner_slots[None, :]
    start, end = (
        jnp.sum(jnp.where(placing, edge[None, :], 0), axis=1) for edge in (doc_starts, doc_ends)
    )
    member = (
        (position[None, :] >= start[:, None]) & (position[None, :] < end[:, None])
    ).astype(jnp.float32)
    arranged = jnp.dot(member, product, precision=lax.Precision.HIGHEST)
    arranged = arranged / jnp.sqrt((end - start).astype(jnp.float32))[:, None]
    per_owner = example_count // lax.axis_size("ex")
    summed = lax.psum(arranged, ("ex", "row"))
    return lax.dynamic_slice_in_dim(summed, lax.axis_index("ex") * per_owner, per_owner, 0)


def solution(mesh):
    sizes = dict(mesh.shape)
    if sizes["row"] == 4:
        body = functools.partial(with_kernel, sizes["ex"])
    else:
        body = with_collectives
    placed = (
        P(("grp", "ex"), "row"),
        P(("grp", "ex"), "row"),
        P("row", None),
        P("row", None),
        P("grp"),
        P("grp"),
    )
    return jax.shard_map(
        body, mesh=mesh, in_specs=placed, out_specs=P(("grp", "ex"), None), check_vma=False
    )
```

```python
import functools

import jax
import jax.numpy as jnp
from jax import lax
from jax.experimental import pallas as pl
from jax.experimental.pallas import tpu as pltpu
from jax.sharding import PartitionSpec as P

MESH = pl.DeviceIdType.MESH
TILE = 256
CHUNK = 64
PER = TILE // CHUNK
RING = 8
LEAD = 4
PEER_LAG = 3
HALVES = 1
LAG = 6


def sums_kernel(
    ex_count, len_ref, own_ref, og_hbm, pg_hbm, hid_hbm, ph_hbm, out_ref,
    og, pg, ph, hid, grad, hidp, near_out, peer_out, near_in, peer_in,
    lo, hi, acc, got_ex, got_row,
    pg_sem, og_sem, ph_sem, hid_sem,
    near_send, near_recv, peer_send, peer_recv, ex_send, ex_recv, row_send, row_recv,
):
    ex = lax.axis_index("ex")
    row = lax.axis_index("row")
    tokens = og_hbm.shape[0]
    tiles = tokens // TILE
    width = og_hbm.shape[1] // PER
    chunks = tokens // CHUNK
    examples = len_ref.shape[1]
    per_owner = examples // ex_count
    depth = ph_hbm.shape[0] // PER
    near = row + 1 - 2 * (row % 2)
    peer = 3 - row
    is_mid = (row == 1) | (row == 2)
    is_end = (row == 0) | (row == 3)

    def load_og(i):
        return pltpu.make_async_copy(
            og_hbm.at[pl.ds(pl.multiple_of(i * TILE, TILE), TILE)], og.at[i], og_sem.at[i]
        )

    def load_ph(k):
        return pltpu.make_async_copy(
            ph_hbm.at[pl.ds(pl.multiple_of(k * depth, depth), depth)], ph.at[k], ph_sem.at[k]
        )

    def load_hid(s):
        i, k = s // PER, s % PER
        return pltpu.make_async_copy(
            hid_hbm.at[
                pl.ds(pl.multiple_of(i * TILE, TILE), TILE),
                pl.ds(pl.multiple_of(k * depth, 128), depth),
            ],
            hid.at[s % RING],
            hid_sem.at[s % RING],
        )

    def near_copy(c):
        return pltpu.make_async_remote_copy(
            src_ref=near_out.at[c], dst_ref=near_in.at[c],
            send_sem=near_send.at[c], recv_sem=near_recv.at[c],
            device_id={"row": near}, device_id_type=MESH,
        )

    def peer_copy(c):
        return pltpu.make_async_remote_copy(
            src_ref=peer_out.at[c], dst_ref=peer_in.at[c],
            send_sem=peer_send.at[c], recv_sem=peer_recv.at[c],
            device_id={"row": peer}, device_id_type=MESH,
        )

    pg_copy = pltpu.make_async_copy(pg_hbm, pg, pg_sem)
    pg_copy.start()
    load_og(0).start()
    load_og(1).start()
    barrier = pltpu.get_barrier_semaphore()
    for d in range(1, ex_count):
        pl.semaphore_signal(barrier, inc=1, device_id={"ex": (ex + d) % ex_count}, device_id_type=MESH)
    for d in range(1, 4):
        pl.semaphore_signal(barrier, inc=1, device_id={"row": (row + d) % 4}, device_id_type=MESH)
    for k in range(PER):
        load_ph(k).start()
        load_hid(k).start()
        if k == 1:
            load_og(2).start()
    for i in range(3, tiles):
        load_og(i).start()
    for s in range(PER, RING):
        load_hid(s).start()

    length = len_ref[...].astype(jnp.float32)
    r = lax.broadcasted_iota(jnp.int32, (examples, examples), 0)
    c = lax.broadcasted_iota(jnp.int32, (examples, examples), 1)
    ends = jnp.sum(jnp.where(c <= r, length, 0.0), axis=1, keepdims=True)
    ends = jnp.sum(jnp.where(r == c, ends, 0.0), axis=0, keepdims=True)
    starts = ends - length
    mine = own_ref[...] == r
    hi[...] = jnp.broadcast_to(
        jnp.sum(jnp.where(mine, ends, 0.0), axis=1, keepdims=True), hi.shape
    )
    lo[...] = jnp.broadcast_to(
        jnp.sum(jnp.where(mine, starts, 0.0), axis=1, keepdims=True), lo.shape
    )
    acc[...] = jnp.zeros_like(acc)

    def grad_tile(i):
        load_og(i).wait()
        g = jnp.dot(og[i], pg[...], preferred_element_type=jnp.float32)
        g = g.reshape(PER, CHUNK, g.shape[-1])
        at = pl.ds(pl.multiple_of(i * PER, PER), PER)
        grad[at] = g

        @pl.when(is_end)
        def _():
            near_out[at] = g.astype(jnp.bfloat16)

    pg_copy.wait()
    grad_tile(0)
    pl.semaphore_wait(barrier, ex_count - 1 + 3)

    @pl.when(is_end)
    def _():
        for m in range(LEAD):
            near_copy(m).start()

    grad_tile(1)

    def add_up(m, total):
        product = total * hidp[m]
        high = product.astype(jnp.bfloat16)
        low = (product - high.astype(jnp.float32)).astype(jnp.bfloat16)
        position = (
            ex * tokens + m * CHUNK + lax.broadcasted_iota(jnp.int32, (examples, CHUNK), 1)
        ).astype(jnp.float32)
        member = jnp.where(
            (position >= lo[:, :CHUNK]) & (position < hi[:, :CHUNK]), 1.0, 0.0
        ).astype(jnp.bfloat16)
        acc[...] += jnp.dot(member, high, preferred_element_type=jnp.float32) + jnp.dot(
            member, low, preferred_element_type=jnp.float32
        )

    def grad_piece(i, k):
        at = pl.ds(pl.multiple_of(i * PER, PER), PER)
        part = pl.ds(pl.multiple_of(k * width, 128), width)
        g = jnp.dot(
            og.at[i][:, part],
            pg[pl.ds(pl.multiple_of(k * width, width), width)],
            preferred_element_type=jnp.float32,
        ).reshape(PER, CHUNK, pg.shape[-1])

        @pl.when(k == 0)
        def _():
            grad[at] = g

        @pl.when(k > 0)
        def _():
            grad[at] += g

        @pl.when(is_end & (k == PER - 1))
        def _():
            near_out[at] = grad[at].astype(jnp.bfloat16)

    def hidden_piece(s, i, k):
        load_hid(s).wait()

        @pl.when(i == 0)
        def _():
            load_ph(k).wait()

        h = jnp.dot(hid[s % RING], ph[k], preferred_element_type=jnp.float32)
        h = h.reshape(PER, CHUNK, h.shape[-1])
        at = pl.ds(pl.multiple_of(i * PER, PER), PER)

        @pl.when(k == 0)
        def _():
            hidp[at] = h

        @pl.when(k > 0)
        def _():
            hidp[at] += h

        @pl.when(s + RING < chunks)
        def _():
            load_hid(s + RING).start()

    def step(s, carry):
        i, k = s // PER, s % PER

        @pl.when(is_mid & (s < chunks))
        def _():
            near_copy(s).wait_recv()
            peer_out[s] = (near_in[s].astype(jnp.float32) + grad[s]).astype(jnp.bfloat16)
            peer_copy(s).start()

        @pl.when(is_mid & (s >= PEER_LAG) & (s < chunks + PEER_LAG))
        def _():
            m = s - PEER_LAG
            peer_copy(m).wait_recv()
            near_out[m] = (peer_in[m].astype(jnp.float32) + grad[m]).astype(jnp.bfloat16)
            near_copy(m).start()

        @pl.when(is_end & (s + LEAD < chunks))
        def _():
            near_copy(s + LEAD).start()

        @pl.when(s < chunks)
        def _():
            hidden_piece(s, i, k)

        @pl.when(i + 2 < tiles)
        def _():
            @pl.when(k == 0)
            def _():
                load_og(i + 2).wait()

            grad_piece(i + 2, k)

        @pl.when(is_end & (s >= LAG))
        def _():
            m = s - LAG
            near_copy(m).wait_recv()
            add_up(m, grad[m] + near_in[m].astype(jnp.float32))

        @pl.when(is_mid & (s >= LAG))
        def _():
            m = s - LAG
            add_up(
                m, grad[m] + near_in[m].astype(jnp.float32) + peer_in[m].astype(jnp.float32)
            )

        return carry

    lax.fori_loop(0, chunks + LAG, step, 0)

    acc[...] = acc[...] / jnp.sqrt(hi[:, :1] - lo[:, :1])
    half = acc.shape[1] // HALVES

    def ex_copy(d, q):
        to = (ex + d) % ex_count
        return pltpu.make_async_remote_copy(
            src_ref=acc.at[
                pl.ds(pl.multiple_of(to * per_owner, per_owner), per_owner),
                pl.ds(q * half, half),
            ],
            dst_ref=got_ex.at[d - 1, :, pl.ds(q * half, half)],
            send_sem=ex_send.at[d - 1, q], recv_sem=ex_recv.at[d - 1, q],
            device_id={"ex": to}, device_id_type=MESH,
        )

    def row_copy(d, q, source):
        return pltpu.make_async_remote_copy(
            src_ref=got_row.at[row, :, pl.ds(q * half, half)],
            dst_ref=got_row.at[source, :, pl.ds(q * half, half)],
            send_sem=row_send.at[d - 1, q], recv_sem=row_recv.at[source, q],
            device_id={"row": (row + d) % 4}, device_id_type=MESH,
        )

    for q in range(HALVES):
        for d in range(1, ex_count):
            ex_copy(d, q).start()
    own_rows = pl.ds(pl.multiple_of(ex * per_owner, per_owner), per_owner)
    for q in range(HALVES):
        at = pl.ds(q * half, half)
        total = acc[own_rows, at]
        for d in range(1, ex_count):
            ex_copy(d, q).wait_recv()
            total = total + got_ex[d - 1, :, at]
        got_row[row, :, at] = total
        for d in range(1, 4):
            row_copy(d, q, row).start()
    for q in range(HALVES):
        at = pl.ds(q * half, half)
        for d in range(1, 4):
            row_copy(d, q, (row + d) % 4).wait_recv()
        out_ref[:, at] = (got_row[0, :, at] + got_row[1, :, at]) + (
            got_row[2, :, at] + got_row[3, :, at]
        )

    for q in range(HALVES):
        for d in range(1, ex_count):
            ex_copy(d, q).wait_send()
        for d in range(1, 4):
            row_copy(d, q, row).wait_send()

    def drain(m, carry):
        near_copy(m).wait_send()

        @pl.when(is_mid)
        def _():
            peer_copy(m).wait_send()

        return carry

    lax.fori_loop(0, chunks, drain, 0)


def with_kernel(ex_count, hidden, out_grads, proj_hidden, proj_grads, lengths, owner_slots):
    tokens, units = hidden.shape
    features = out_grads.shape[1]
    k_dim = proj_hidden.shape[1]
    examples = lengths.shape[0]
    per_owner = examples // ex_count
    tiles, chunks = tokens // TILE, tokens // CHUNK
    bf16, f32 = jnp.bfloat16, jnp.float32
    dma = pltpu.SemaphoreType.DMA
    messages = pltpu.VMEM((chunks, CHUNK, k_dim), bf16)
    return pl.pallas_call(
        functools.partial(sums_kernel, ex_count),
        out_shape=jax.ShapeDtypeStruct((per_owner, k_dim), f32),
        in_specs=[pl.BlockSpec(memory_space=pltpu.VMEM)] * 2
        + [pl.BlockSpec(memory_space=pl.ANY)] * 4,
        out_specs=pl.BlockSpec(memory_space=pltpu.VMEM),
        scratch_shapes=[
            pltpu.VMEM((tiles, TILE, features), bf16),
            pltpu.VMEM((features, k_dim), bf16),
            pltpu.VMEM((PER, units // PER, k_dim), bf16),
            pltpu.VMEM((RING, TILE, units // PER), bf16),
            pltpu.VMEM((chunks, CHUNK, k_dim), f32),
            pltpu.VMEM((chunks, CHUNK, k_dim), f32),
            messages, messages, messages, messages,
            pltpu.VMEM((examples, 128), f32),
            pltpu.VMEM((examples, 128), f32),
            pltpu.VMEM((examples, k_dim), f32),
            pltpu.VMEM((ex_count - 1, per_owner, k_dim), f32),
            pltpu.VMEM((4, per_owner, k_dim), f32),
            dma, dma((tiles,)), dma((PER,)), dma((RING,)),
            dma((chunks,)), dma((chunks,)), dma((chunks,)), dma((chunks,)),
            dma((ex_count - 1, HALVES)), dma((ex_count - 1, HALVES)), dma((3, HALVES)), dma((4, HALVES)),
        ],
        compiler_params=pltpu.CompilerParams(
            collective_id=0, has_side_effects=True, vmem_limit_bytes=56 * 2**20
        ),
    )(lengths[None, :], owner_slots[None, :], out_grads, proj_grads, hidden, proj_hidden)


def with_collectives(hidden, out_grads, proj_hidden, proj_grads, lengths, owner_slots):
    tok_count = hidden.shape[0]
    example_count = lengths.shape[0]
    shares = lax.psum_scatter(
        jnp.dot(out_grads, proj_grads, preferred_element_type=jnp.float32),
        "row",
        scatter_dimension=0,
        tiled=True,
    )
    shares_low = shares.astype(jnp.bfloat16)
    hid_part = jnp.dot(hidden, proj_hidden, preferred_element_type=jnp.float32)
    doc_ends = jnp.cumsum(lengths)
    doc_starts = doc_ends - lengths
    grad_proj = lax.all_gather(shares_low, "row", axis=0, tiled=True)
    product = hid_part * grad_proj.astype(jnp.float32)
    position = lax.axis_index("ex") * tok_count + jnp.arange(tok_count, dtype=jnp.int32)
    slot_ids = jnp.arange(example_count, dtype=jnp.int32)
    placing = slot_ids[:, None] == owner_slots[None, :]
    start, end = (
        jnp.sum(jnp.where(placing, edge[None, :], 0), axis=1) for edge in (doc_starts, doc_ends)
    )
    member = (
        (position[None, :] >= start[:, None]) & (position[None, :] < end[:, None])
    ).astype(jnp.float32)
    arranged = jnp.dot(member, product, precision=lax.Precision.HIGHEST)
    arranged = arranged / jnp.sqrt((end - start).astype(jnp.float32))[:, None]
    per_owner = example_count // lax.axis_size("ex")
    summed = lax.psum(arranged, ("ex", "row"))
    return lax.dynamic_slice_in_dim(summed, lax.axis_index("ex") * per_owner, per_owner, 0)


def solution(mesh):
    sizes = dict(mesh.shape)
    if sizes["row"] == 4:
        body = functools.partial(with_kernel, sizes["ex"])
    else:
        body = with_collectives
    placed = (
        P(("grp", "ex"), "row"),
        P(("grp", "ex"), "row"),
        P("row", None),
        P("row", None),
        P("grp"),
        P("grp"),
    )
    return jax.shard_map(
        body, mesh=mesh, in_specs=placed, out_specs=P(("grp", "ex"), None), check_vma=False
    )
```
